256 devices in a mesh: row: 8 (over x, core), col: 32 (over y, z).
Axes of the slice: x: 4, y: 4, z: 8, core: 2. Of those that a mesh axis runs over, the one named last changes fastest.
Arguments:
- hamiltonian: bfloat16 [7, 16, 32, 128, 128], P(None, 'row', 'col'), may hold values from -0.09375 to 0.09375
- term_prev: bfloat16 [7, 16, 32, 128, 128], P(None, 'row', 'col'), may hold values from -6 to 6
- term_now: bfloat16 [7, 16, 32, 128, 128], P(None, 'row', 'col'), may hold values from -6 to 6
- pattern: int32 [7, 16, 32], P(None, 'row', 'col'), may hold values from 0 to 1, as said below
- weights: float32 [12], replicated, may hold values from 0.5 to 1.5
Outputs:
- density: float32 [7, 16, 32, 128, 128], P(None, 'row', 'col')
- term_before: bfloat16 [7, 16, 32, 128, 128], P(None, 'row', 'col')
- term_last: bfloat16 [7, 16, 32, 128, 128], P(None, 'row', 'col')
The draws below stay inside these ranges and needn't reach their ends.
Inputs may be any that keep to these rules, and one draw needn't show every extreme that they name: `pattern`: the offset-zero entries (index 3) are always 1; about three quarters of the others are 1.
All inputs are finite; a program needn't handle non-finite values.
Results may differ from the reference program's by a relative error of at most 0.011.
Values may be sent and summed in bfloat16 or wider, within the bound.
No kernel may reach another device: no remote copies, remote signals or barrier semaphores. Data moves between devices by JAX's collectives and lax.ppermute only.
A program may use at most 64 MiB of HBM per device.

```python
import jax
import jax.numpy as jnp

BLOCK = 128
BAND = 3
OFFSETS = 7
TERMS = 12
ROWS_DEV = 2
NBLOCKS = 512
N_ROW = 8
N_COL = 32


def draw_pattern(key, part):
    key = jax.random.fold_in(key, 7)
    levels = jax.random.randint(key, (OFFSETS, N_ROW * ROWS_DEV, N_COL), 0, 4)
    pattern = jnp.where(levels > 0, 1, 0).astype(jnp.int32)
    return pattern.at[BAND].set(1)


def level_of(own_key, shape, cuts, least, largest):
    def one(position, parts):
        steps = jax.random.uniform(jax.random.fold_in(jax.random.fold_in(own_key, 6), position), (parts,), jnp.float32, least / len(cuts), largest / len(cuts))
        return jnp.repeat(jnp.exp(steps), shape[position] // parts).reshape((-1,) + (1,) * (len(shape) - position - 1))

    level = one(*cuts[0])
    for cut in cuts[1:]:
        level = level * one(*cut)
    return level


def gaussian(stream_key, extent, deviation, most, shards=(), held_as=jnp.bfloat16):
    drawn = deviation * jax.random.normal(stream_key, extent, jnp.float32)
    if shards:
        drawn = drawn * level_of(stream_key, extent, shards, -0.22, 0.18)
    return jnp.clip(drawn, -most, most).astype(held_as)


def setup_inputs(seed: int = 0) -> dict:
    streams_of = jax.random.split(jax.random.key(seed), 6)
    hamiltonian = gaussian(streams_of[0], (OFFSETS, N_ROW * ROWS_DEV, N_COL, BLOCK, BLOCK), (4 * OFFSETS * BLOCK) ** -0.5, 0.09375, ((1, 8), (2, 32)))
    term_prev = gaussian(streams_of[1], (OFFSETS, N_ROW * ROWS_DEV, N_COL, BLOCK, BLOCK), 1.0, 6.0, ((1, 8), (2, 32)))
    term_now = gaussian(streams_of[2], (OFFSETS, N_ROW * ROWS_DEV, N_COL, BLOCK, BLOCK), 1.0, 6.0, ((1, 8), (2, 32)))
    pattern = draw_pattern(jax.random.fold_in(streams_of[5], 71), 0)
    weights = jnp.clip(jax.random.uniform(streams_of[4], (TERMS,), jnp.float32, 0.5, 1.5), 0.5, 1.5)
    return dict(hamiltonian=hamiltonian, term_prev=term_prev, term_now=term_now, pattern=pattern, weights=weights)


def band_product(term_band, ham_band, live_mask):
    results = []
    for offset in range(-BAND, BAND + 1):
        accum = jnp.zeros(term_band.shape[1:], jnp.float32)
        for shift_by in range(max(-BAND, offset - BAND), min(BAND, offset + BAND) + 1):
            left_part = term_band[shift_by + BAND].astype(jnp.float32)
            right_part = jnp.roll(ham_band[offset - shift_by + BAND], -shift_by, axis=0).astype(jnp.float32)
            accum = accum + jnp.einsum('ixy,iyz->ixz', left_part, right_part)
        results.append(accum)
    return jnp.stack(results) * live_mask[:, :, None, None]


def reference(hamiltonian, term_prev, term_now, pattern, weights):
    out_shape = hamiltonian.shape
    live_mask = pattern.reshape(OFFSETS, NBLOCKS).astype(jnp.float32)

    def to_band(array):
        return array.reshape(OFFSETS, NBLOCKS, BLOCK, BLOCK).astype(jnp.float32) * live_mask[:, :, None, None]

    ham_band = to_band(hamiltonian).astype(jnp.bfloat16)
    older = to_band(term_prev)
    newer = to_band(term_now).astype(jnp.bfloat16)
    density = jnp.zeros((OFFSETS, NBLOCKS, BLOCK, BLOCK), jnp.float32)
    for step in range(TERMS):
        product = band_product(newer, ham_band, live_mask)
        following = 2.0 * product - older
        density = density + weights[step] * following
        older = newer.astype(jnp.float32)
        newer = following.astype(jnp.bfloat16)
    return (density.reshape(out_shape), older.astype(jnp.bfloat16).reshape(out_shape), newer.reshape(out_shape))
```

```python
import functools

import jax
import jax.numpy as jnp
from jax import lax
from jax.experimental import pallas as pl
from jax.experimental.pallas import tpu as pltpu
from jax.sharding import PartitionSpec as P

BAND = 3
TERMS = 12
GROUPS = ((0, 2), (2, 4), (4, 6), (6, 7))


def towards_lower(rows, cols, slot):
    pairs = []
    for r in range(rows):
        for c in range(cols):
            if c > 0:
                dst = r * cols + c - 1
            else:
                dst = ((r - 1 + slot) % rows) * cols + cols - 1
            pairs.append((r * cols + c, dst))
    return pairs


def towards_upper(rows, cols, slot):
    pairs = []
    for r in range(rows):
        for c in range(cols):
            if c < cols - 1:
                dst = r * cols + c + 1
            else:
                dst = ((r + slot) % rows) * cols
            pairs.append((r * cols + c, dst))
    return pairs


def terms_kernel(weights, scale, swaps, own, prev, now, *refs):
    rows, block = 2, own.shape[-1]
    offsets = own.shape[0]
    after = refs[: BAND * rows]
    before = refs[BAND * rows : 2 * BAND * rows]
    density, out_before, out_last, table, older, newer, total, sems = refs[2 * BAND * rows :]

    def cols(o):
        return slice(o * block, (o + 1) * block)

    for row in range(rows):
        table[row, cols(4), cols(0)] = jnp.zeros((block, block), jnp.bfloat16)
        table[row, cols(6), cols(2)] = jnp.zeros((block, block), jnp.bfloat16)
        table[row, cols(1), cols(5)] = jnp.zeros((block, block), jnp.bfloat16)
        for o in range(offsets):
            table[row, cols(BAND), cols(o)] = own[o, row]
        for dist in range(1, BAND + 1):
            for side in range(2):
                slabs = (after, before)[side]
                swapped = swaps[side * BAND + dist - 1] > 0
                for flip in range(2):
                    slab = slabs[(dist - 1) * rows + (row ^ flip)]

                    @pl.when(swapped if flip else jnp.logical_not(swapped))
                    def _():
                        for k in range(offsets - dist):
                            if side == 0:
                                table[row, cols(BAND + dist), cols(dist + k)] = slab[k]
                            else:
                                table[row, cols(BAND - dist), cols(offsets - 1 - dist - k)] = slab[k]

        for o in range(offsets):
            live = scale[row, o] > 0.0
            older[row, :, cols(o)] = jnp.where(live, prev[o, row], jnp.zeros((), jnp.bfloat16))
            newer[row, :, cols(o)] = jnp.where(live, now[o, row], jnp.zeros((), jnp.bfloat16))

    def term(step, cur, oth, first, last):
        weight = weights[step]
        for row in range(rows):
            for low, high in GROUPS:
                start, stop = max(0, low - BAND), min(offsets, high + BAND)
                product = jnp.dot(
                    cur[row, :, start * block : stop * block],
                    table[row, start * block : stop * block, low * block : high * block],
                    preferred_element_type=jnp.float32,
                )
                for o in range(low, high):
                    part = product[:, (o - low) * block : (o - low + 1) * block]
                    following = scale[row, o] * part - oth[row, :, cols(o)].astype(jnp.float32)
                    if first:
                        total[o, row] = weight * following
                    else:
                        total[o, row] += weight * following
                    oth[row, :, cols(o)] = following.astype(jnp.bfloat16)
                    if last:
                        copy_out(0, o, row).start()
                        copy_out(2, o, row).start()

    def copy_out(which, o, row):
        if which == 0:
            return pltpu.make_async_copy(total.at[o, row], density.at[o, row], sems.at[0, row, o])
        src = older if which == 1 else newer
        dst = out_before if which == 1 else out_last
        return pltpu.make_async_copy(src.at[row, :, cols(o)], dst.at[o, row], sems.at[which, row, o])

    term(0, newer, older, True, False)

    def pair(i, carry):
        term(2 * i + 1, older, newer, False, False)
        term(2 * i + 2, newer, older, False, False)
        return carry

    lax.fori_loop(0, (TERMS - 2) // 2, pair, 0)
    for row in range(rows):
        for o in range(offsets):
            copy_out(1, o, row).start()
    term(TERMS - 1, older, newer, False, True)
    for which in range(3):
        for row in range(rows):
            for o in range(offsets):
                copy_out(which, o, row).wait()


def body(hamiltonian, term_prev, term_now, pattern, weights):
    out_shape = hamiltonian.shape
    offsets, rows, block = out_shape[0], out_shape[1], out_shape[3]
    band_shape = (offsets, rows, block, block)
    row_count, col_count = lax.axis_size("row"), lax.axis_size("col")
    col = lax.axis_index("col")
    live = pattern.reshape(offsets, rows)
    own = hamiltonian.reshape(band_shape) * live.astype(jnp.bfloat16)[:, :, None, None]
    lower = [towards_lower(row_count, col_count, slot) for slot in range(rows)]
    upper = [towards_upper(row_count, col_count, slot) for slot in range(rows)]
    down = [own[: offsets - 1, slot] for slot in range(rows)]
    up = [own[:0:-1, slot] for slot in range(rows)]
    after, before = [], []
    for dist in range(1, BAND + 1):
        for slot in range(rows):
            down[slot] = lax.ppermute(down[slot][: offsets - dist], ("row", "col"), lower[slot])
            up[slot] = lax.ppermute(up[slot][: offsets - dist], ("row", "col"), upper[slot])
        after += down
        before += up
    swaps = jnp.stack(
        [col + dist >= col_count for dist in range(1, BAND + 1)]
        + [col < dist for dist in range(1, BAND + 1)]
    ).astype(jnp.int32)
    scale = 2.0 * live.T.astype(jnp.float32)

    vmem = pl.BlockSpec(memory_space=pltpu.VMEM)
    smem = pl.BlockSpec(memory_space=pltpu.SMEM)
    hbm = pl.BlockSpec(memory_space=pl.ANY)
    density, last_but_one, last = pl.pallas_call(
        terms_kernel,
        out_shape=(
            jax.ShapeDtypeStruct(band_shape, jnp.float32),
            jax.ShapeDtypeStruct(band_shape, jnp.bfloat16),
            jax.ShapeDtypeStruct(band_shape, jnp.bfloat16),
        ),
        in_specs=[smem] * 3 + [vmem] * (3 + len(after) + len(before)),
        out_specs=(hbm, hbm, hbm),
        scratch_shapes=[
            pltpu.VMEM((rows, offsets * block, offsets * block), jnp.bfloat16),
            pltpu.VMEM((rows, block, offsets * block), jnp.bfloat16),
            pltpu.VMEM((rows, block, offsets * block), jnp.bfloat16),
            pltpu.VMEM(band_shape, jnp.float32),
            pltpu.SemaphoreType.DMA((3, rows, offsets)),
        ],
        compiler_params=pltpu.CompilerParams(vmem_limit_bytes=32 * 2**20),
        cost_estimate=pl.CostEstimate(
            flops=2 * TERMS * rows * 37 * block**3, bytes_accessed=6 * 2**20, transcendentals=0
        ),
    )(
        weights,
        scale,
        swaps,
        own,
        term_prev.reshape(band_shape),
        term_now.reshape(band_shape),
        *after,
        *before,
    )
    return density.reshape(out_shape), last_but_one.reshape(out_shape), last.reshape(out_shape)


def solution(mesh):
    placed = P(None, "row", "col", None, None)
    return jax.shard_map(
        body,
        mesh=mesh,
        in_specs=(placed, placed, placed, P(None, "row", "col"), P()),
        out_specs=(placed, placed, placed),
        check_vma=False,
    )
```

```python
import functools

import jax
import jax.numpy as jnp
from jax import lax
from jax.experimental import pallas as pl
from jax.experimental.pallas import tpu as pltpu
from jax.sharding import PartitionSpec as P

BAND = 3
TERMS = 12
GROUPS = ((0, 2), (2, 4), (4, 6), (6, 7))


def even_first(rows, cols):
    return [(r * cols + c, r * cols + (c ^ 1)) for r in range(rows) for c in range(cols)]


def odd_first(rows, cols, slot):
    pairs = []
    for r in range(rows):
        for c in range(cols):
            if c % 2 == 1:
                dst = r * cols + c + 1 if c < cols - 1 else ((r + slot) % rows) * cols
            else:
                dst = r * cols + c - 1 if c > 0 else ((r - 1 + slot) % rows) * cols + cols - 1
            pairs.append((r * cols + c, dst))
    return pairs


def live_or_zero(live, block):
    return jnp.where(live, block, jnp.zeros((), block.dtype))


def mirror(offsets):
    odd = lax.rem(lax.axis_index("col"), 2)
    return lambda o: o + odd * (offsets - 1 - 2 * o)


def twice_or_zero(live, block):
    return live_or_zero(live, block + block)


def alive(pattern):
    offsets, rows = pattern.shape
    stored = mirror(offsets)
    return [[pattern[stored(o), row] > 0 for o in range(offsets)] for row in range(rows)]


def place(table, live, row, dist, side, slabs):
    offsets, block = 2 * BAND + 1, slabs[0].shape[-1]
    col, last = lax.axis_index("col"), lax.axis_size("col") - 1
    towards_last = lax.rem(col, 2) == side
    swapped = jnp.where(towards_last, last - col, col) < dist
    a = BAND + dist if side == 0 else BAND - dist
    for k in range(offsets - dist):
        o = dist + k if side == 0 else offsets - 1 - dist - k
        table[row, a * block : (a + 1) * block, o * block : (o + 1) * block] = twice_or_zero(
            live[row][o], jnp.where(swapped, slabs[1 - row][k], slabs[row][k])
        )


def start_kernel(pattern, weights, ham, prev, now, *refs):
    rows, offsets, block = 2, ham.shape[0], ham.shape[-1]
    near, far = refs[: (BAND - 1) * rows], refs[(BAND - 1) * rows : 2 * (BAND - 1) * rows]
    table, older, newer, tiles, got, scalars, sems = refs[2 * (BAND - 1) * rows :]
    stored = mirror(offsets)
    live = alive(pattern)

    def cols(o):
        return slice(o * block, (o + 1) * block)

    fetch = [pltpu.make_async_copy(src, got.at[i], sems.at[i]) for i, src in enumerate((ham, prev, now))]
    fetch.append(pltpu.make_async_copy(weights, scalars, sems.at[3]))
    for copy in fetch:
        copy.start()
    for row in range(rows):
        for a, o in ((4, 0), (1, 5)):
            table[row, cols(a), cols(o)] = jnp.zeros((block, block), jnp.bfloat16)
        for dist in range(1, BAND):
            for side, slabs in enumerate((near, far)):
                place(table, live, row, dist, side, slabs[(dist - 1) * rows : dist * rows])
    for copy in fetch:
        copy.wait()
    for row in range(rows):
        for o in range(offsets):
            at = stored(o)
            table[row, cols(BAND), cols(o)] = twice_or_zero(live[row][o], got[0, at, row])
            older[row, :, cols(o)] = live_or_zero(live[row][o], got[1, at, row])
            newer[row, :, cols(o)] = live_or_zero(live[row][o], got[2, at, row])
    for step in range(TERMS):
        tiles[step] = jnp.full(tiles.shape[1:], scalars[step])


def terms_kernel(pattern, near, near1, far, far1, tiles, table_in, older_in, newer_in, *refs):
    density, out_before, out_last, table, older, newer, total, out_sems = refs
    older[...] = older_in[...]
    newer[...] = newer_in[...]
    offsets, rows, block = total.shape[:3]
    stored = mirror(offsets)
    live = alive(pattern)

    def cols(o):
        return slice(o * block, (o + 1) * block)

    for row in range(rows):
        for a, start, stop in ((1, 0, 6), (2, 0, 6), (3, 0, 7), (4, 0, 7), (5, 2, 7)):
            part = (row, cols(a), slice(start * block, stop * block))
            table[part] = table_in[part]
        table[row, cols(6), cols(2)] = jnp.zeros((block, block), jnp.bfloat16)
        place(table, live, row, BAND, 0, (near, near1))
        place(table, live, row, BAND, 1, (far, far1))

    def copy_out(which, o, row):
        if which == 0:
            return pltpu.make_async_copy(total.at[o, row], density.at[stored(o), row], out_sems.at[0, row, o])
        src = older if which == 1 else newer
        dst = out_before if which == 1 else out_last
        return pltpu.make_async_copy(src.at[row, :, cols(o)], dst.at[stored(o), row], out_sems.at[which, row, o])

    for step in range(TERMS):
        cur, oth = (newer, older) if step % 2 == 0 else (older, newer)
        weight = tiles[step, :1]
        last = step == TERMS - 1
        for row in range(rows):
            for low, high in GROUPS:
                start, stop = max(0, low - BAND), min(offsets, high + BAND)
                product = jnp.dot(
                    cur[row, :, start * block : stop * block],
                    table[row, start * block : stop * block, low * block : high * block],
                    preferred_element_type=jnp.float32,
                )
                for o in range(low, high):
                    part = product[:, (o - low) * block : (o - low + 1) * block]
                    following = part - oth[row, :, cols(o)].astype(jnp.float32)
                    if step == 0:
                        total[o, row] = weight * following
                    else:
                        total[o, row] += weight * following
                    oth[row, :, cols(o)] = following.astype(jnp.bfloat16)
                    if last:
                        copy_out(0, o, row).start()
                        copy_out(2, o, row).start()
        if step == TERMS - 2:
            for row in range(rows):
                for o in range(offsets):
                    copy_out(1, o, row).start()
    for which in range(3):
        for row in range(rows):
            for o in range(offsets):
                copy_out(which, o, row).wait()


def body(hamiltonian, term_prev, term_now, pattern, weights):
    out_shape = hamiltonian.shape
    offsets, rows, block = out_shape[0], out_shape[1], out_shape[3]
    band_shape = (offsets, rows, block, block)
    row_count, col_count = lax.axis_size("row"), lax.axis_size("col")
    live = pattern.reshape(offsets, rows)
    vmem = pl.BlockSpec(memory_space=pltpu.VMEM)
    smem = pl.BlockSpec(memory_space=pltpu.SMEM)
    hbm = pl.BlockSpec(memory_space=pltpu.HBM)
    ham = hamiltonian.reshape(band_shape)
    kept = jnp.where(live[:, :, None, None] > 0, ham, jnp.zeros((), ham.dtype))
    odd = lax.axis_index("col") % 2 == 1
    low, high = kept[: offsets - 1], kept[:0:-1]
    pairs = even_first(row_count, col_count)
    across = [odd_first(row_count, col_count, slot) for slot in range(rows)]
    axes = ("row", "col")
    to_far = [jnp.where(odd, high[:, slot], low[:, slot]) for slot in range(rows)]
    to_near = [jnp.where(odd, low[:, slot], high[:, slot]) for slot in range(rows)]
    near, far = [], []
    for dist in range(1, BAND + 1):
        from_far, from_near = [], []
        for slot in range(rows):
            from_far.append(lax.ppermute(to_far[slot][: offsets - dist], axes, across[slot]))
            from_near.append(lax.ppermute(to_near[slot][: offsets - dist], axes, pairs))
        near += from_near
        far += from_far
        to_far, to_near = from_near, from_far

    table = jax.ShapeDtypeStruct((rows, offsets * block, offsets * block), jnp.bfloat16)
    term = jax.ShapeDtypeStruct((rows, block, offsets * block), jnp.bfloat16)
    held = (BAND - 1) * rows
    *begun, tiles = pl.pallas_call(
        start_kernel,
        out_shape=(table, term, term, jax.ShapeDtypeStruct((TERMS, 8, block), jnp.float32)),
        in_specs=[smem] + [hbm] * 4 + [vmem] * (2 * held),
        out_specs=(vmem,) * 4,
        scratch_shapes=[
            pltpu.VMEM((3, *band_shape), jnp.bfloat16),
            pltpu.SMEM((TERMS,), jnp.float32),
            pltpu.SemaphoreType.DMA((4,)),
        ],
        compiler_params=pltpu.CompilerParams(vmem_limit_bytes=10 * 2**20),
        cost_estimate=pl.CostEstimate(flops=0, bytes_accessed=4 * 2**20, transcendentals=0),
    )(
        live,
        weights,
        ham,
        term_prev.reshape(band_shape),
        term_now.reshape(band_shape),
        *near[:held],
        *far[:held],
    )
    density, last_but_one, last, *_ = pl.pallas_call(
        terms_kernel,
        out_shape=(
            jax.ShapeDtypeStruct(band_shape, jnp.float32),
            jax.ShapeDtypeStruct(band_shape, jnp.bfloat16),
            jax.ShapeDtypeStruct(band_shape, jnp.bfloat16),
        ),
        in_specs=[smem] + [vmem] * 8,
        out_specs=(hbm, hbm, hbm),
        scratch_shapes=[
            pltpu.VMEM(table.shape, table.dtype),
            pltpu.VMEM(term.shape, term.dtype),
            pltpu.VMEM(term.shape, term.dtype),
            pltpu.VMEM(band_shape, jnp.float32),
            pltpu.SemaphoreType.DMA((3, rows, offsets)),
        ],
        compiler_params=pltpu.CompilerParams(vmem_limit_bytes=10 * 2**20),
        cost_estimate=pl.CostEstimate(
            flops=2 * TERMS * rows * 37 * block**3, bytes_accessed=6 * 2**20, transcendentals=0
        ),
    )(live, *near[held:], *far[held:], tiles, *begun)
    return density.reshape(out_shape), last_but_one.reshape(out_shape), last.reshape(out_shape)


def solution(mesh):
    placed = P(None, "row", "col", None, None)
    return jax.shard_map(
        body,
        mesh=mesh,
        in_specs=(placed, placed, placed, P(None, "row", "col"), P()),
        out_specs=(placed, placed, placed),
        check_vma=False,
    )
```

```python
import functools

import jax
import jax.numpy as jnp
from jax import lax
from jax.experimental import pallas as pl
from jax.experimental.pallas import tpu as pltpu
from jax.sharding import PartitionSpec as P

BAND = 3
TERMS = 12
LEAST = 5
GROUPS = ((0, 2), (2, 4), (4, 6), (6, 7))


def even_first(rows, cols):
    return [(r * cols + c, r * cols + (c ^ 1)) for r in range(rows) for c in range(cols)]


def odd_first(rows, cols, slot):
    pairs = []
    for r in range(rows):
        for c in range(cols):
            if c % 2 == 1:
                dst = r * cols + c + 1 if c < cols - 1 else ((r + slot) % rows) * cols
            else:
                dst = r * cols + c - 1 if c > 0 else ((r - 1 + slot) % rows) * cols + cols - 1
            pairs.append((r * cols + c, dst))
    return pairs


def live_or_zero(live, block):
    return jnp.where(live, block, jnp.zeros((), block.dtype))


def mirror(offsets):
    odd = lax.rem(lax.axis_index("col"), 2)
    return lambda o: o + odd * (offsets - 1 - 2 * o)


def twice_or_zero(live, block):
    return live_or_zero(live, block + block)


def alive(pattern):
    offsets, rows = pattern.shape
    stored = mirror(offsets)
    return [[pattern[stored(o), row] > 0 for o in range(offsets)] for row in range(rows)]


def place(table, live, row, dist, side, slabs):
    offsets, block = 2 * BAND + 1, slabs[0].shape[-1]
    col, last = lax.axis_index("col"), lax.axis_size("col") - 1
    towards_last = lax.rem(col, 2) == side
    swapped = jnp.where(towards_last, last - col, col) < dist
    a = BAND + dist if side == 0 else BAND - dist
    for k in range(offsets - dist):
        o = dist + k if side == 0 else offsets - 1 - dist - k
        table[row, a * block : (a + 1) * block, o * block : (o + 1) * block] = twice_or_zero(
            live[row][o], jnp.where(swapped, slabs[1 - row][k], slabs[row][k])
        )


def start_kernel(pattern, weights, ham, prev, now, *refs):
    rows, offsets, block = 2, ham.shape[0], ham.shape[-1]
    near, far = refs[: (BAND - 1) * rows], refs[(BAND - 1) * rows : 2 * (BAND - 1) * rows]
    table, older, newer, tiles, scalars, sem = refs[2 * (BAND - 1) * rows :]
    stored = mirror(offsets)
    live = alive(pattern)

    def cols(o):
        return slice(o * block, (o + 1) * block)

    fetch = pltpu.make_async_copy(weights, scalars, sem)
    fetch.start()
    for row in range(rows):
        for a, o in ((4, 0), (1, 5)):
            table[row, cols(a), cols(o)] = jnp.zeros((block, block), jnp.bfloat16)
        for dist in range(1, BAND):
            for side, slabs in enumerate((near, far)):
                place(table, live, row, dist, side, slabs[(dist - 1) * rows : dist * rows])
    for row in range(rows):
        for o in range(offsets):
            at = stored(o)
            table[row, cols(BAND), cols(o)] = twice_or_zero(live[row][o], ham[at, row])
            older[row, :, cols(o)] = live_or_zero(live[row][o], prev[at, row])
            newer[row, :, cols(o)] = live_or_zero(live[row][o], now[at, row])
    fetch.wait()
    for step in range(TERMS):
        tiles[step] = jnp.full(tiles.shape[1:], scalars[step])


def terms_kernel(pattern, near, near1, far, far1, tiles, table_in, older_in, newer_in, *refs):
    density, out_before, out_last, table, older, newer, total, out_sems = refs
    older[...] = older_in[...]
    newer[...] = newer_in[...]
    offsets, rows, block = total.shape[:3]
    stored = mirror(offsets)
    live = alive(pattern)

    def cols(o):
        return slice(o * block, (o + 1) * block)

    def fill(row):
        for a, start, stop in ((1, 0, 6), (2, 0, 6), (3, 0, 7), (4, 0, 7), (5, 2, 7)):
            part = (row, cols(a), slice(start * block, stop * block))
            table[part] = table_in[part]
        table[row, cols(6), cols(2)] = jnp.zeros((block, block), jnp.bfloat16)
        place(table, live, row, BAND, 0, (near, near1))
        place(table, live, row, BAND, 1, (far, far1))

    def copy_out(which, o, row):
        if which == 0:
            return pltpu.make_async_copy(total.at[o, row], density.at[stored(o), row], out_sems.at[0, row, o])
        src = older if which == 1 else newer
        dst = out_before if which == 1 else out_last
        return pltpu.make_async_copy(src.at[row, :, cols(o)], dst.at[stored(o), row], out_sems.at[which, row, o])

    def term(row, step):
        cur, oth = (newer, older) if step % 2 == 0 else (older, newer)
        weight = tiles[step, :1]
        for low, high in GROUPS:
            start, stop = max(0, low - BAND), min(offsets, high + BAND)
            product = jnp.dot(
                cur[row, :, start * block : stop * block],
                table[row, start * block : stop * block, low * block : high * block],
                preferred_element_type=jnp.float32,
            )
            for o in range(low, high):
                part = product[:, (o - low) * block : (o - low + 1) * block]
                following = part - oth[row, :, cols(o)].astype(jnp.float32)
                if step == 0:
                    total[o, row] = weight * following
                else:
                    total[o, row] += weight * following
                oth[row, :, cols(o)] = following.astype(jnp.bfloat16)
                if step == TERMS - 1:
                    copy_out(0, o, row).start()
                    copy_out(2, o, row).start()
        if step == TERMS - 2:
            for o in range(offsets):
                copy_out(1, o, row).start()

    for step in range(TERMS):
        for row in range(rows):
            if step == 0:
                fill(row)
            term(row, step)
    for which in range(3):
        for row in range(rows):
            for o in range(offsets):
                copy_out(which, o, row).wait()


def body(hamiltonian, term_prev, term_now, pattern, weights):
    out_shape = hamiltonian.shape
    offsets, rows, block = out_shape[0], out_shape[1], out_shape[3]
    band_shape = (offsets, rows, block, block)
    row_count, col_count = lax.axis_size("row"), lax.axis_size("col")
    live = pattern.reshape(offsets, rows)
    vmem = pl.BlockSpec(memory_space=pltpu.VMEM)
    smem = pl.BlockSpec(memory_space=pltpu.SMEM)
    hbm = pl.BlockSpec(memory_space=pltpu.HBM)
    ham = hamiltonian.reshape(band_shape)
    kept = ham * live.astype(ham.dtype)[:, :, None, None]
    odd = lax.axis_index("col") % 2 == 1
    low, high = kept[: offsets - 1], kept[:0:-1]
    pairs = even_first(row_count, col_count)
    across = [odd_first(row_count, col_count, slot) for slot in range(rows)]
    axes = ("row", "col")
    to_far = [jnp.where(odd, high[:, slot], low[:, slot]) for slot in range(rows)]
    to_near = [jnp.where(odd, low[:, slot], high[:, slot]) for slot in range(rows)]
    near, far = [], []
    for dist in range(1, BAND + 1):
        from_far, from_near = [], []
        for slot in range(rows):
            from_far.append(lax.ppermute(to_far[slot][: max(offsets - dist, LEAST)], axes, across[slot]))
            from_near.append(lax.ppermute(to_near[slot][: max(offsets - dist, LEAST)], axes, pairs))
        near += from_near
        far += from_far
        to_far, to_near = from_near, from_far

    table = jax.ShapeDtypeStruct((rows, offsets * block, offsets * block), jnp.bfloat16)
    term = jax.ShapeDtypeStruct((rows, block, offsets * block), jnp.bfloat16)
    held = (BAND - 1) * rows
    *begun, tiles = pl.pallas_call(
        start_kernel,
        out_shape=(table, term, term, jax.ShapeDtypeStruct((TERMS, 8, block), jnp.float32)),
        in_specs=[smem, hbm] + [vmem] * (3 + 2 * held),
        out_specs=(vmem,) * 4,
        scratch_shapes=[
            pltpu.SMEM((TERMS,), jnp.float32),
            pltpu.SemaphoreType.DMA,
        ],
        compiler_params=pltpu.CompilerParams(vmem_limit_bytes=10 * 2**20),
        cost_estimate=pl.CostEstimate(flops=0, bytes_accessed=4 * 2**20, transcendentals=0),
    )(
        live,
        weights,
        ham,
        term_prev.reshape(band_shape),
        term_now.reshape(band_shape),
        *near[:held],
        *far[:held],
    )
    density, last_but_one, last, *_ = pl.pallas_call(
        terms_kernel,
        out_shape=(
            jax.ShapeDtypeStruct(band_shape, jnp.float32),
            jax.ShapeDtypeStruct(band_shape, jnp.bfloat16),
            jax.ShapeDtypeStruct(band_shape, jnp.bfloat16),
        ),
        in_specs=[smem] + [vmem] * 8,
        out_specs=(hbm, hbm, hbm),
        scratch_shapes=[
            pltpu.VMEM(table.shape, table.dtype),
            pltpu.VMEM(term.shape, term.dtype),
            pltpu.VMEM(term.shape, term.dtype),
            pltpu.VMEM(band_shape, jnp.float32),
            pltpu.SemaphoreType.DMA((3, rows, offsets)),
        ],
        compiler_params=pltpu.CompilerParams(vmem_limit_bytes=10 * 2**20),
        cost_estimate=pl.CostEstimate(
            flops=2 * TERMS * rows * 37 * block**3, bytes_accessed=6 * 2**20, transcendentals=0
        ),
    )(live, *near[held:], *far[held:], tiles, *begun)
    return density.reshape(out_shape), last_but_one.reshape(out_shape), last.reshape(out_shape)


def solution(mesh):
    placed = P(None, "row", "col", None, None)
    return jax.shard_map(
        body,
        mesh=mesh,
        in_specs=(placed, placed, placed, P(None, "row", "col"), P()),
        out_specs=(placed, placed, placed),
        check_vma=False,
    )
```

```python
import functools

import jax
import jax.numpy as jnp
from jax import lax
from jax.experimental import pallas as pl
from jax.experimental.pallas import tpu as pltpu
from jax.sharding import PartitionSpec as P

BAND = 3
TERMS = 12
GROUPS = ((0, 2), (2, 4), (4, 6), (6, 7))


def even_first(rows, cols):
    return [(r * cols + c, r * cols + (c ^ 1)) for r in range(rows) for c in range(cols)]


def odd_first(rows, cols, slot):
    pairs = []
    for r in range(rows):
        for c in range(cols):
            if c % 2 == 1:
                dst = r * cols + c + 1 if c < cols - 1 else ((r + slot) % rows) * cols
            else:
                dst = r * cols + c - 1 if c > 0 else ((r - 1 + slot) % rows) * cols + cols - 1
            pairs.append((r * cols + c, dst))
    return pairs


def live_or_zero(live, block):
    return jnp.where(live, block, jnp.zeros((), block.dtype))


def mirror(offsets):
    odd = lax.rem(lax.axis_index("col"), 2)
    return lambda o: o + odd * (offsets - 1 - 2 * o)


def twice_or_zero(live, block):
    return live_or_zero(live, block + block)


def alive(pattern):
    offsets, rows = pattern.shape
    stored = mirror(offsets)
    return [[pattern[stored(o), row] > 0 for o in range(offsets)] for row in range(rows)]


def place(table, live, row, dist, side, slabs):
    offsets, block = 2 * BAND + 1, slabs[0].shape[-1]
    col, last = lax.axis_index("col"), lax.axis_size("col") - 1
    towards_last = lax.rem(col, 2) == side
    swapped = jnp.where(towards_last, last - col, col) < dist
    a = BAND + dist if side == 0 else BAND - dist
    for k in range(offsets - dist):
        o = dist + k if side == 0 else offsets - 1 - dist - k
        table[row, a * block : (a + 1) * block, o * block : (o + 1) * block] = twice_or_zero(
            live[row][o], jnp.where(swapped, slabs[1 - row][k], slabs[row][k])
        )


def start_kernel(pattern, weights, ham, prev, now, *refs):
    rows, offsets, block = 2, ham.shape[0], ham.shape[-1]
    near, far = refs[: (BAND - 1) * rows], refs[(BAND - 1) * rows : 2 * (BAND - 1) * rows]
    table, older, newer, tiles, scalars, sem = refs[2 * (BAND - 1) * rows :]
    stored = mirror(offsets)
    live = alive(pattern)

    def cols(o):
        return slice(o * block, (o + 1) * block)

    fetch = pltpu.make_async_copy(weights, scalars, sem)
    fetch.start()
    for row in range(rows):
        for a, o in ((4, 0), (1, 5)):
            table[row, cols(a), cols(o)] = jnp.zeros((block, block), jnp.bfloat16)
        for dist in range(1, BAND):
            for side, slabs in enumerate((near, far)):
                place(table, live, row, dist, side, slabs[(dist - 1) * rows : dist * rows])
    for row in range(rows):
        for o in range(offsets):
            at = stored(o)
            table[row, cols(BAND), cols(o)] = twice_or_zero(live[row][o], ham[at, row])
            older[row, :, cols(o)] = live_or_zero(live[row][o], prev[at, row])
            newer[row, :, cols(o)] = live_or_zero(live[row][o], now[at, row])
    fetch.wait()
    for step in range(TERMS):
        tiles[step] = jnp.full(tiles.shape[1:], scalars[step])


def terms_kernel(pattern, near, near1, far, far1, tiles, table_in, older_in, newer_in, *refs):
    density, out_before, out_last, table, older, newer, total, out_sems = refs
    older[...] = older_in[...]
    newer[...] = newer_in[...]
    offsets, rows, block = total.shape[:3]
    stored = mirror(offsets)
    live = alive(pattern)

    def cols(o):
        return slice(o * block, (o + 1) * block)

    def fill(row):
        for a, start, stop in ((1, 0, 6), (2, 0, 6), (3, 0, 7), (4, 0, 7), (5, 2, 7)):
            part = (row, cols(a), slice(start * block, stop * block))
            table[part] = table_in[part]
        table[row, cols(6), cols(2)] = jnp.zeros((block, block), jnp.bfloat16)
        place(table, live, row, BAND, 0, (near, near1))
        place(table, live, row, BAND, 1, (far, far1))

    def copy_out(which, o, row):
        if which == 0:
            return pltpu.make_async_copy(total.at[o, row], density.at[stored(o), row], out_sems.at[0, row, o])
        src = older if which == 1 else newer
        dst = out_before if which == 1 else out_last
        return pltpu.make_async_copy(src.at[row, :, cols(o)], dst.at[stored(o), row], out_sems.at[which, row, o])

    def term(row, step):
        cur, oth = (newer, older) if step % 2 == 0 else (older, newer)
        weight = tiles[step, :1]
        for low, high in GROUPS:
            start, stop = max(0, low - BAND), min(offsets, high + BAND)
            product = jnp.dot(
                cur[row, :, start * block : stop * block],
                table[row, start * block : stop * block, low * block : high * block],
                preferred_element_type=jnp.float32,
            )
            for o in range(low, high):
                part = product[:, (o - low) * block : (o - low + 1) * block]
                following = part - oth[row, :, cols(o)].astype(jnp.float32)
                if step == 0:
                    total[o, row] = weight * following
                else:
                    total[o, row] += weight * following
                oth[row, :, cols(o)] = following.astype(jnp.bfloat16)
                if step == TERMS - 1:
                    copy_out(0, o, row).start()
                    copy_out(2, o, row).start()
        if step == TERMS - 2:
            for o in range(offsets):
                copy_out(1, o, row).start()

    for step in range(TERMS):
        for row in range(rows):
            if step == 0:
                fill(row)
            term(row, step)
    for which in range(3):
        for row in range(rows):
            for o in range(offsets):
                copy_out(which, o, row).wait()


def body(hamiltonian, term_prev, term_now, pattern, weights):
    out_shape = hamiltonian.shape
    offsets, rows, block = out_shape[0], out_shape[1], out_shape[3]
    band_shape = (offsets, rows, block, block)
    row_count, col_count = lax.axis_size("row"), lax.axis_size("col")
    live = pattern.reshape(offsets, rows)
    vmem = pl.BlockSpec(memory_space=pltpu.VMEM)
    smem = pl.BlockSpec(memory_space=pltpu.SMEM)
    hbm = pl.BlockSpec(memory_space=pltpu.HBM)
    ham = hamiltonian.reshape(band_shape)
    kept = ham * live.astype(ham.dtype)[:, :, None, None]
    odd = lax.axis_index("col") % 2 == 1
    low, high = kept[: offsets - 1], kept[:0:-1]
    pairs = even_first(row_count, col_count)
    across = [odd_first(row_count, col_count, slot) for slot in range(rows)]
    axes = ("row", "col")
    to_far = [jnp.where(odd, high[:, slot], low[:, slot]) for slot in range(rows)]
    to_near = [jnp.where(odd, low[:, slot], high[:, slot]) for slot in range(rows)]
    near, far = [], []
    for dist in range(1, BAND + 1):
        from_far, from_near = [], []
        for slot in range(rows):
            from_far.append(lax.ppermute(to_far[slot][: offsets - dist], axes, across[slot]))
            from_near.append(lax.ppermute(to_near[slot][: offsets - dist], axes, pairs))
        near += from_near
        far += from_far
        to_far, to_near = from_near, from_far

    table = jax.ShapeDtypeStruct((rows, offsets * block, offsets * block), jnp.bfloat16)
    term = jax.ShapeDtypeStruct((rows, block, offsets * block), jnp.bfloat16)
    held = (BAND - 1) * rows
    *begun, tiles = pl.pallas_call(
        start_kernel,
        out_shape=(table, term, term, jax.ShapeDtypeStruct((TERMS, 8, block), jnp.float32)),
        in_specs=[smem, hbm] + [vmem] * (3 + 2 * held),
        out_specs=(vmem,) * 4,
        scratch_shapes=[
            pltpu.SMEM((TERMS,), jnp.float32),
            pltpu.SemaphoreType.DMA,
        ],
        compiler_params=pltpu.CompilerParams(vmem_limit_bytes=10 * 2**20),
        cost_estimate=pl.CostEstimate(flops=0, bytes_accessed=4 * 2**20, transcendentals=0),
    )(
        live,
        weights,
        ham,
        term_prev.reshape(band_shape),
        term_now.reshape(band_shape),
        *near[:held],
        *far[:held],
    )
    density, last_but_one, last, *_ = pl.pallas_call(
        terms_kernel,
        out_shape=(
            jax.ShapeDtypeStruct(band_shape, jnp.float32),
            jax.ShapeDtypeStruct(band_shape, jnp.bfloat16),
            jax.ShapeDtypeStruct(band_shape, jnp.bfloat16),
        ),
        in_specs=[smem] + [vmem] * 8,
        out_specs=(hbm, hbm, hbm),
        scratch_shapes=[
            pltpu.VMEM(table.shape, table.dtype),
            pltpu.VMEM(term.shape, term.dtype),
            pltpu.VMEM(term.shape, term.dtype),
            pltpu.VMEM(band_shape, jnp.float32),
            pltpu.SemaphoreType.DMA((3, rows, offsets)),
        ],
        compiler_params=pltpu.CompilerParams(vmem_limit_bytes=10 * 2**20),
        cost_estimate=pl.CostEstimate(
            flops=2 * TERMS * rows * 37 * block**3, bytes_accessed=6 * 2**20, transcendentals=0
        ),
    )(live, *near[held:], *far[held:], tiles, *begun)
    return density.reshape(out_shape), last_but_one.reshape(out_shape), last.reshape(out_shape)


def solution(mesh):
    placed = P(None, "row", "col", None, None)
    return jax.shard_map(
        body,
        mesh=mesh,
        in_specs=(placed, placed, placed, P(None, "row", "col"), P()),
        out_specs=(placed, placed, placed),
        check_vma=False,
    )
```

```python
import functools

import jax
import jax.numpy as jnp
from jax import lax
from jax.experimental import pallas as pl
from jax.experimental.pallas import tpu as pltpu
from jax.sharding import PartitionSpec as P

BAND = 3
TERMS = 12
GROUPS = ((0, 2), (2, 4), (4, 6), (6, 7))


def even_first(rows, cols):
    return [(r * cols + c, r * cols + (c ^ 1)) for r in range(rows) for c in range(cols)]


def odd_first(rows, cols, slot):
    pairs = []
    for r in range(rows):
        for c in range(cols):
            if c % 2 == 1:
                dst = r * cols + c + 1 if c < cols - 1 else ((r + slot) % rows) * cols
            else:
                dst = r * cols + c - 1 if c > 0 else ((r - 1 + slot) % rows) * cols + cols - 1
            pairs.append((r * cols + c, dst))
    return pairs


def live_or_zero(live, block):
    return jnp.where(live, block, jnp.zeros((), block.dtype))


def mirror(offsets):
    odd = lax.rem(lax.axis_index("col"), 2)
    return lambda o: o + odd * (offsets - 1 - 2 * o)


def twice_or_zero(live, block):
    return live_or_zero(live, block + block)


def alive(pattern):
    offsets, rows = pattern.shape
    stored = mirror(offsets)
    return [[pattern[stored(o), row] > 0 for o in range(offsets)] for row in range(rows)]


def place(table, live, row, dist, side, slabs):
    offsets, block = 2 * BAND + 1, slabs[0].shape[-1]
    col, last = lax.axis_index("col"), lax.axis_size("col") - 1
    towards_last = lax.rem(col, 2) == side
    swapped = jnp.where(towards_last, last - col, col) < dist
    a = BAND + dist if side == 0 else BAND - dist
    for k in range(offsets - dist):
        o = dist + k if side == 0 else offsets - 1 - dist - k
        table[row, a * block : (a + 1) * block, o * block : (o + 1) * block] = twice_or_zero(
            live[row][o], jnp.where(swapped, slabs[1 - row][k], slabs[row][k])
        )


def start_kernel(pattern, weights, ham, prev, now, *refs):
    rows, offsets, block = 2, ham.shape[0], ham.shape[-1]
    near, far = refs[: (BAND - 1) * rows], refs[(BAND - 1) * rows : 2 * (BAND - 1) * rows]
    table, older, newer, tiles, scalars, sem = refs[2 * (BAND - 1) * rows :]
    stored = mirror(offsets)
    live = alive(pattern)

    def cols(o):
        return slice(o * block, (o + 1) * block)

    fetch = pltpu.make_async_copy(weights, scalars, sem)
    fetch.start()
    for row in range(rows):
        for a, o in ((4, 0), (1, 5)):
            table[row, cols(a), cols(o)] = jnp.zeros((block, block), jnp.bfloat16)
        for dist in range(1, BAND):
            for side, slabs in enumerate((near, far)):
                place(table, live, row, dist, side, slabs[(dist - 1) * rows : dist * rows])
    for row in range(rows):
        for o in range(offsets):
            at = stored(o)
            table[row, cols(BAND), cols(o)] = twice_or_zero(live[row][o], ham[at, row])
            older[row, :, cols(o)] = live_or_zero(live[row][o], prev[at, row])
            newer[row, :, cols(o)] = live_or_zero(live[row][o], now[at, row])
    fetch.wait()
    for step in range(TERMS):
        tiles[step] = jnp.full(tiles.shape[1:], scalars[step])


def terms_kernel(pattern, near, near1, far, far1, tiles, table_in, older_in, newer_in, *refs):
    density, out_before, out_last, table, older, newer, total, out_sems = refs
    offsets, rows, block = total.shape[:3]
    stored = mirror(offsets)
    live = alive(pattern)

    def cols(o):
        return slice(o * block, (o + 1) * block)

    def fill(row):
        older[row] = older_in[row]
        newer[row] = newer_in[row]
        for a, start, stop in ((1, 0, 6), (2, 0, 6), (3, 0, 7), (4, 0, 7), (5, 2, 7)):
            part = (row, cols(a), slice(start * block, stop * block))
            table[part] = table_in[part]
        table[row, cols(6), cols(2)] = jnp.zeros((block, block), jnp.bfloat16)
        place(table, live, row, BAND, 0, (near, near1))
        place(table, live, row, BAND, 1, (far, far1))

    def copy_out(which, o, row):
        if which == 0:
            return pltpu.make_async_copy(total.at[o, row], density.at[stored(o), row], out_sems.at[0, row, o])
        src = older if which == 1 else newer
        dst = out_before if which == 1 else out_last
        return pltpu.make_async_copy(src.at[row, :, cols(o)], dst.at[stored(o), row], out_sems.at[which, row, o])

    def term(row, step):
        cur, oth = (newer, older) if step % 2 == 0 else (older, newer)
        weight = tiles[step, :1]
        for low, high in GROUPS:
            start, stop = max(0, low - BAND), min(offsets, high + BAND)
            product = jnp.dot(
                cur[row, :, start * block : stop * block],
                table[row, start * block : stop * block, low * block : high * block],
                preferred_element_type=jnp.float32,
            )
            for o in range(low, high):
                part = product[:, (o - low) * block : (o - low + 1) * block]
                following = part - oth[row, :, cols(o)].astype(jnp.float32)
                if step == 0:
                    total[o, row] = weight * following
                else:
                    total[o, row] += weight * following
                oth[row, :, cols(o)] = following.astype(jnp.bfloat16)
                if step == TERMS - 1:
                    copy_out(0, o, row).start()
                    copy_out(2, o, row).start()
        if step == TERMS - 2:
            for o in range(offsets):
                copy_out(1, o, row).start()

    for step in range(TERMS):
        for row in range(rows):
            if step == 0:
                fill(row)
            term(row, step)
    for which in range(3):
        for row in range(rows):
            for o in range(offsets):
                copy_out(which, o, row).wait()


def body(hamiltonian, term_prev, term_now, pattern, weights):
    out_shape = hamiltonian.shape
    offsets, rows, block = out_shape[0], out_shape[1], out_shape[3]
    band_shape = (offsets, rows, block, block)
    row_count, col_count = lax.axis_size("row"), lax.axis_size("col")
    live = pattern.reshape(offsets, rows)
    vmem = pl.BlockSpec(memory_space=pltpu.VMEM)
    smem = pl.BlockSpec(memory_space=pltpu.SMEM)
    hbm = pl.BlockSpec(memory_space=pltpu.HBM)
    ham = hamiltonian.reshape(band_shape)
    kept = ham * live.astype(ham.dtype)[:, :, None, None]
    odd = lax.axis_index("col") % 2 == 1
    low, high = kept[: offsets - 1], kept[:0:-1]
    pairs = even_first(row_count, col_count)
    across = [odd_first(row_count, col_count, slot) for slot in range(rows)]
    axes = ("row", "col")
    to_far = [jnp.where(odd, high[:, slot], low[:, slot]) for slot in range(rows)]
    to_near = [jnp.where(odd, low[:, slot], high[:, slot]) for slot in range(rows)]
    near, far = [], []
    for dist in range(1, BAND + 1):
        from_far, from_near = [], []
        for slot in range(rows):
            from_far.append(lax.ppermute(to_far[slot][: offsets - dist], axes, across[slot]))
            from_near.append(lax.ppermute(to_near[slot][: offsets - dist], axes, pairs))
        near += from_near
        far += from_far
        to_far, to_near = from_near, from_far

    table = jax.ShapeDtypeStruct((rows, offsets * block, offsets * block), jnp.bfloat16)
    term = jax.ShapeDtypeStruct((rows, block, offsets * block), jnp.bfloat16)
    held = (BAND - 1) * rows
    *begun, tiles = pl.pallas_call(
        start_kernel,
        out_shape=(table, term, term, jax.ShapeDtypeStruct((TERMS, 8, block), jnp.float32)),
        in_specs=[smem, hbm] + [vmem] * (3 + 2 * held),
        out_specs=(vmem,) * 4,
        scratch_shapes=[
            pltpu.SMEM((TERMS,), jnp.float32),
            pltpu.SemaphoreType.DMA,
        ],
        compiler_params=pltpu.CompilerParams(vmem_limit_bytes=10 * 2**20),
        cost_estimate=pl.CostEstimate(flops=0, bytes_accessed=4 * 2**20, transcendentals=0),
    )(
        live,
        weights,
        ham,
        term_prev.reshape(band_shape),
        term_now.reshape(band_shape),
        *near[:held],
        *far[:held],
    )
    density, last_but_one, last, *_ = pl.pallas_call(
        terms_kernel,
        out_shape=(
            jax.ShapeDtypeStruct(band_shape, jnp.float32),
            jax.ShapeDtypeStruct(band_shape, jnp.bfloat16),
            jax.ShapeDtypeStruct(band_shape, jnp.bfloat16),
        ),
        in_specs=[smem] + [vmem] * 8,
        out_specs=(hbm, hbm, hbm),
        scratch_shapes=[
            pltpu.VMEM(table.shape, table.dtype),
            pltpu.VMEM(term.shape, term.dtype),
            pltpu.VMEM(term.shape, term.dtype),
            pltpu.VMEM(band_shape, jnp.float32),
            pltpu.SemaphoreType.DMA((3, rows, offsets)),
        ],
        compiler_params=pltpu.CompilerParams(vmem_limit_bytes=10 * 2**20),
        cost_estimate=pl.CostEstimate(
            flops=2 * TERMS * rows * 37 * block**3, bytes_accessed=6 * 2**20, transcendentals=0
        ),
    )(live, *near[held:], *far[held:], tiles, *begun)
    return density.reshape(out_shape), last_but_one.reshape(out_shape), last.reshape(out_shape)


def solution(mesh):
    placed = P(None, "row", "col", None, None)
    return jax.shard_map(
        body,
        mesh=mesh,
        in_specs=(placed, placed, placed, P(None, "row", "col"), P()),
        out_specs=(placed, placed, placed),
        check_vma=False,
    )
```
